32 devices in a mesh: af: 4 (over y, x), sa: 8 (over z, core).
Axes of the slice: x: 2, y: 2, z: 4, core: 2. Of those that a mesh axis runs over, the one named last changes fastest.
Arguments:
- pressure: bfloat16 [4, 32, 1024, 2048], P(None, 'af', 'sa'), may hold values from -6 to 6
- legendre: bfloat16 [512, 1025, 512], P(('af', 'sa')), may hold values from -0.1875 to 0.1875
- radial: bfloat16 [1024, 32, 128], replicated, may hold values from -1 to 1
Outputs:
- shells: bfloat16 [512, 1025, 2, 4, 128], P(('af', 'sa'))
The draws below stay inside these ranges and needn't reach their ends.
All inputs are finite; a program needn't handle non-finite values.
Results may differ from the reference program's by a relative error of at most 0.0071.
Values may be sent and summed in bfloat16 or wider, within the bound.
No kernel may reach another device: no remote copies, remote signals or barrier semaphores. Data moves between devices by JAX's collectives and lax.ppermute only.
A program may use at most 448 MiB of HBM per device.

```python
import math
import jax
import jax.numpy as jnp
from jax import lax

NLAT = 1024
NLON = 2048
LDEG = 1024
SHELLS = 128
FRAMES = 4
FREQS = 32
PAIRS = 512


def steps_of(stream_key, shape, shards, low, top_value):
    factor_of, own = 1.0, jax.random.fold_in(stream_key, 6)
    for axis_at, parts in shards:
        draws = jnp.exp(jax.random.uniform(jax.random.fold_in(own, axis_at), (parts,), jnp.float32, low / len(shards), top_value / len(shards)))
        factor_of = factor_of * jnp.repeat(draws, shape[axis_at] // parts).reshape([-1 if axis == axis_at else 1 for axis in range(len(shape))])
    return factor_of


def scatter_about(own_key, extent, spread, most, pieces=(), kind=jnp.bfloat16):
    array = jax.random.normal(own_key, extent, jnp.float32) * spread
    if len(pieces) > 0:
        array = steps_of(own_key, extent, pieces, -0.22, 0.18) * array
    return jnp.clip(array, min=-most, max=most).astype(kind)


def setup_inputs(seed: int = 0) -> dict:
    streams_of = jax.random.split(jax.random.key(seed), 4)
    pressure = scatter_about(streams_of[0], (FRAMES, FREQS, NLAT, NLON), 1.0, 6.0, ((1, 4), (2, 8)))
    legendre = scatter_about(streams_of[1], (PAIRS, LDEG + 1, NLAT // 2), NLAT ** -0.5, 0.1875, ((0, 32),))
    radial = scatter_about(streams_of[2], (LDEG, FREQS, SHELLS), FREQS ** -0.5, 1.0)
    return {"pressure": pressure, "legendre": legendre, "radial": radial}


def order_of_column(column_count):
    column = lax.iota(jnp.int32, column_count)
    halves = column // 2
    return jnp.where(column % 2 == 0, halves, LDEG - 1 - halves)

def fourier_table(lon_count, orders):
    longitude = lax.iota(jnp.int32, lon_count)
    product = longitude[:, None] * orders[None, :] % lon_count
    phases = product.astype(jnp.float32) * (2.0 * math.pi / lon_count)
    norm_scale = 1.0 / math.sqrt(lon_count)
    return jnp.stack([jnp.cos(phases) * norm_scale, -jnp.sin(phases) * norm_scale], axis=1).astype(jnp.bfloat16)

def pair_layout(pair_index):
    column = lax.iota(jnp.int32, LDEG + 1)
    segment = (column >= LDEG - pair_index).astype(jnp.int32)
    order_here = jnp.where(segment == 1, LDEG - 1 - pair_index, pair_index)
    degree = jnp.where(segment == 1, column - 1, pair_index + column)
    parity = (degree + order_here) % 2
    return (segment, degree, parity)

def selector(segment, parity):
    branch_ids = lax.iota(jnp.int32, 2)
    seg_match = segment[..., None, None, :] == branch_ids[:, None, None]
    par_match = parity[..., None, None, :] == branch_ids[None, :, None]
    return (seg_match & par_match).astype(jnp.float32)

def reference(pressure, legendre, radial):
    frames, freqs, lat_count, lon_count = pressure.shape
    trig_table = fourier_table(lon_count, order_of_column(LDEG))
    spectra = jnp.einsum('krc,xfjk->rcxfj', trig_table.astype(jnp.float32), pressure.astype(jnp.float32)).astype(jnp.bfloat16)
    half_count = lat_count // 2
    upper_half = spectra[..., :half_count].astype(jnp.float32)
    lower_half = jnp.flip(spectra[..., half_count:], axis=4).astype(jnp.float32)
    even_part = (upper_half + lower_half).astype(jnp.bfloat16)
    odd_part = (upper_half - lower_half).astype(jnp.bfloat16)
    folded = jnp.stack([even_part, odd_part], axis=2)
    folded = folded.reshape(2, LDEG // 2, 2, 2, frames, freqs, half_count)

    def one_pair(pair_index):
        piece = lax.dynamic_index_in_dim(folded, pair_index, 1, keepdims=False)
        weights = lax.dynamic_index_in_dim(legendre, pair_index, 0, keepdims=False)
        products = jnp.einsum('rstxfj,qj->rstxfq', piece.astype(jnp.float32), weights.astype(jnp.float32))
        segment, degree, parity = pair_layout(pair_index)
        select = selector(segment, parity)
        harmonic = lax.optimization_barrier(jnp.sum(products * select[None, :, :, None, None, :], axis=(1, 2))).astype(jnp.bfloat16)
        factors = jnp.take(radial, degree, axis=0)
        result = jnp.einsum('rxfq,qfs->qrxs', harmonic.astype(jnp.float32), factors.astype(jnp.float32))
        return result.astype(jnp.bfloat16)
    return lax.map(one_pair, jnp.arange(LDEG // 2, dtype=jnp.int32))
```

```python
import math

import jax
import jax.numpy as jnp
import numpy as np
from jax import lax
from jax.experimental import pallas as pl
from jax.experimental.pallas import tpu as pltpu
from jax.sharding import PartitionSpec as P

LDEG = 1024
CHUNKS = (2, 5, 5, 3, 1)
VMEM_LIMIT = 62 * 1024 * 1024


def order_of_column(column_count):
    column = lax.iota(jnp.int32, column_count)
    halves = column // 2
    return jnp.where(column % 2 == 0, halves, LDEG - 1 - halves)


def fourier_table(lon_count, orders):
    longitude = lax.iota(jnp.int32, lon_count)
    product = longitude[:, None] * orders[None, :] % lon_count
    phases = product.astype(jnp.float32) * (2.0 * math.pi / lon_count)
    norm_scale = 1.0 / math.sqrt(lon_count)
    return jnp.stack([jnp.cos(phases) * norm_scale, -jnp.sin(phases) * norm_scale], axis=1).astype(
        jnp.bfloat16
    )


def pair_layout(pair_index):
    column = lax.iota(jnp.int32, LDEG + 1)
    segment = (column >= LDEG - pair_index).astype(jnp.int32)
    order_here = jnp.where(segment == 1, LDEG - 1 - pair_index, pair_index)
    degree = jnp.where(segment == 1, column - 1, pair_index + column)
    parity = (degree + order_here) % 2
    return (segment, degree, parity)


def selector(segment, parity):
    branch_ids = lax.iota(jnp.int32, 2)
    seg_match = segment[..., None, None, :] == branch_ids[:, None, None]
    par_match = parity[..., None, None, :] == branch_ids[None, :, None]
    return (seg_match & par_match).astype(jnp.float32)


def harmonics(gathered, legendre, select):
    parts, per_device, frame_count, freqs, lat_count = gathered.shape
    half_count = lat_count // 2
    upper_half = gathered[..., :half_count].astype(jnp.float32)
    lower_half = jnp.flip(gathered[..., half_count:], axis=4).astype(jnp.float32)
    even_part = (upper_half + lower_half).astype(jnp.bfloat16)
    odd_part = (upper_half - lower_half).astype(jnp.bfloat16)
    folded = jnp.stack([even_part, odd_part], axis=2)
    folded = folded.reshape(parts, per_device // 2, 2, 2, frame_count, freqs, half_count)
    products = jnp.einsum(
        "rkstxfj,kqj->krstxfq", folded, legendre, preferred_element_type=jnp.float32
    )
    return jnp.sum(products * select[:, None, :, :, None, None, :], axis=(2, 3)).astype(
        jnp.bfloat16
    )


def plain_on_device(pressure, legendre, radial):
    frames, freq_dev, lat_dev, lon_count = pressure.shape
    af_count = lax.axis_size("af")
    sa_count = lax.axis_size("sa")
    per_device = LDEG // (af_count * sa_count)
    trig_table = fourier_table(lon_count, order_of_column(LDEG))
    spectra = jnp.einsum(
        "krc,xfjk->rcxfj", trig_table, pressure, preferred_element_type=jnp.float32
    ).astype(jnp.bfloat16)
    pairs_here = legendre.shape[0]
    owner_block = lax.axis_index("af") * sa_count + lax.axis_index("sa")
    pair_ids = owner_block * pairs_here + lax.iota(jnp.int32, pairs_here)
    segment, degree, parity = pair_layout(pair_ids[:, None])
    select = selector(segment, parity)
    spread = spectra.reshape(1, 2, af_count * sa_count, per_device, frames, freq_dev, lat_dev)
    piece = lax.all_to_all(spread, ("af", "sa"), split_axis=2, concat_axis=0, tiled=True)
    frame_count = piece.shape[4]
    sources = piece.reshape(af_count, sa_count, 2, per_device, frame_count, freq_dev, lat_dev)
    sources = jnp.transpose(sources, (2, 3, 4, 0, 5, 1, 6))
    gathered = sources.reshape(2, per_device, frame_count, af_count * freq_dev, sa_count * lat_dev)
    harmonic = harmonics(gathered, legendre, select)
    factors = jnp.take(radial, degree.reshape(-1), axis=0)
    factors = factors.reshape(pairs_here, LDEG + 1, radial.shape[1], radial.shape[2])
    result = jnp.einsum("krxfq,kqfs->kqrxs", harmonic, factors, preferred_element_type=jnp.float32)
    return result.astype(jnp.bfloat16)


def table_rows(lon_count, devices, pairs_here, first, count):
    pair = np.arange(devices)[:, None] * pairs_here + first + np.arange(count)[None, :]
    order = np.stack([pair, LDEG - 1 - pair], axis=1)
    product = (order[..., None].astype(np.int64) * np.arange(lon_count)) % lon_count
    phase = product.astype(np.float32) * np.float32(2.0 * math.pi / lon_count)
    scale = np.float32(1.0 / math.sqrt(lon_count))
    rows = np.stack([np.cos(phase) * scale, -np.sin(phase) * scale], axis=1)
    return rows.reshape(devices * 4 * count, lon_count).astype(jnp.bfloat16)


def dot_t(a, b):
    return lax.dot_general(a, b, (((1,), (1,)), ((), ())), preferred_element_type=jnp.float32)


def dft_kernel(table_ref, pressure_ref, out_ref, acc_ref):
    rows = table_ref.shape[0]
    frame = pl.program_id(0)
    for f in range(0, 8, 2):
        block = pressure_ref[0, f : f + 2].reshape(256, pressure_ref.shape[3])
        both = dot_t(table_ref[...], block)
        at = (frame % 2) * 8 + f
        acc_ref[pl.ds(at, rows, stride=16), :] = both[:, :128]
        acc_ref[pl.ds(at + 1, rows, stride=16), :] = both[:, 128:]

    @pl.when(frame % 2 == 1)
    def _():
        out_ref[...] = acc_ref[...].reshape(rows, 16, 128).astype(jnp.bfloat16)


def dft(table, pressure):
    rows, lon_count = table.shape
    return pl.pallas_call(
        dft_kernel,
        grid=(4,),
        in_specs=[
            pl.BlockSpec((rows, lon_count), lambda x: (0, 0), pipeline_mode=pl.Buffered(1)),
            pl.BlockSpec((1, 8, 128, lon_count), lambda x: (x, 0, 0, 0)),
        ],
        out_specs=pl.BlockSpec((rows, 16, 128), lambda x: (0, x // 2, 0)),
        out_shape=jax.ShapeDtypeStruct((rows, 32, 128), jnp.bfloat16),
        scratch_shapes=[pltpu.VMEM((rows * 16, 128), jnp.float32)],
        compiler_params=pltpu.CompilerParams(vmem_limit_bytes=VMEM_LIMIT),
        cost_estimate=pl.CostEstimate(
            flops=2 * rows * 4096 * lon_count, bytes_accessed=1 << 24, transcendentals=0
        ),
        name="dft_piece",
    )(table, pressure)


def shells_kernel(first, *refs):
    base_ref, recv_ref, leg_ref, rad_ref, pick_ref, flip_ref = refs[:6]
    out_ref, both_ref, harm_ref, copies_ref, result_ref = refs[-5:]
    pair = base_ref[0] + first + pl.program_id(0)
    bound = LDEG - pair

    for s in range(4):
        lanes = slice(128 * s, 128 * s + 128)
        for seg in range(2):
            mirrored = []
            for r in range(2):
                for a in range(4):
                    row = 128 * r + 32 * a
                    both_ref[seg, row : row + 32, lanes] = recv_ref[8 * a + s, r, seg, 0]
                    mirrored.append(recv_ref[8 * a + 7 - s, r, seg, 0])
            mirrored = jnp.concatenate(mirrored, axis=0)
            turned = jnp.dot(mirrored, flip_ref[...], preferred_element_type=jnp.float32)
            both_ref[seg, 256:512, lanes] = turned.astype(jnp.bfloat16)

    own_q = (
        lax.broadcasted_iota(jnp.int32, (64, 256), 1) // 32
        == lax.broadcasted_iota(jnp.int32, (64, 256), 0) % 8
    )

    def legendre_rows(rows, start, seg):
        product = dot_t(rows, both_ref[seg])
        q = start + lax.broadcasted_iota(jnp.int32, (rows.shape[0], 256), 0)
        parity = (q + seg * pair) % 2
        north, south = product[:, :256], product[:, 256:]
        return q, north + jnp.where(parity == 0, south, -south)

    def degree(q):
        return jnp.where(q >= bound, q - 1, pair + q)

    def factors_at(degree_here):
        return rad_ref[pl.ds(pl.multiple_of(degree_here * 32, 32), 32), :]

    def fill_copies(harm):
        harm = harm.astype(jnp.bfloat16)
        for rx in range(8):
            copies_ref[rx, 0 : harm.shape[0]] = jnp.dot(
                harm, pick_ref[rx], preferred_element_type=jnp.float32
            )

    def radial_block(block, slab):
        rows = [copies_ref[rx, 8 * block : 8 * block + 8] for rx in range(8)]
        diagonal = jnp.where(own_q, jnp.concatenate(rows, axis=0), 0.0).astype(jnp.bfloat16)
        result = jnp.dot(diagonal, slab, preferred_element_type=jnp.float32)
        for rx in range(8):
            result_ref[pl.ds(64 * block + rx, 8, stride=8), :] = result[8 * rx : 8 * rx + 8]

    @pl.loop(0, 8)
    def _(tile):
        start = pl.multiple_of(tile * 128, 128)
        rows = leg_ref[0, pl.ds(start, 128), :]

        @pl.when(start < bound)
        def _():
            _, harm = legendre_rows(rows, start, 0)
            harm_ref[...] = harm

        @pl.when(start + 128 > bound)
        def _():
            q, harm = legendre_rows(rows, start, 1)
            harm_ref[...] = jnp.where(q >= bound, harm, harm_ref[...])

        fill_copies(harm_ref[...])
        for block in range(16):
            slab = [factors_at(degree(start + 8 * block + k)) for k in range(8)]
            radial_block(block, jnp.concatenate(slab, axis=0))
        at = pl.multiple_of(start * 8, 1024)
        out_ref[0, pl.ds(at, 1024), :] = result_ref[...].astype(jnp.bfloat16)

    rows = jnp.broadcast_to(leg_ref[0, LDEG : LDEG + 1, :].astype(jnp.float32), (16, 512))
    _, harm = legendre_rows(rows.astype(jnp.bfloat16), LDEG, 1)
    fill_copies(jnp.broadcast_to(harm[0:1], (16, 256)))
    radial_block(0, jnp.concatenate([factors_at(LDEG - 1)] * 8, axis=0))
    out_ref[0, 8 * LDEG : 8 * LDEG + 8, :] = result_ref[0:8].astype(jnp.bfloat16)


def shells_piece(base, received, legendre, radial, pick, flip, output, first, count):
    pairs_here = legendre.shape[0]
    rows = 8 * (LDEG + 1)
    once = pl.Buffered(1)
    in_specs = [
        pl.BlockSpec(memory_space=pltpu.SMEM),
        pl.BlockSpec((32, 2, 2, 1, 32, 128), lambda i: (0, 0, 0, i, 0, 0)),
        pl.BlockSpec((1, LDEG + 1, 512), lambda i: (first + i, 0, 0)),
        pl.BlockSpec(radial.shape, lambda i: (0, 0), pipeline_mode=once),
        pl.BlockSpec((8, 256, 256), lambda i: (0, 0, 0)),
        pl.BlockSpec((128, 128), lambda i: (0, 0)),
    ]
    operands = [base, received, legendre, radial, pick, flip]
    aliases = {}
    if output is not None:
        in_specs.append(pl.BlockSpec(memory_space=pl.ANY))
        operands.append(output)
        aliases = {6: 0}

    def kernel(*refs):
        shells_kernel(first, *refs)

    return pl.pallas_call(
        kernel,
        grid=(count,),
        in_specs=in_specs,
        out_specs=pl.BlockSpec((1, rows, 128), lambda i: (first + i, 0, 0)),
        out_shape=jax.ShapeDtypeStruct((pairs_here, rows, 128), jnp.bfloat16),
        scratch_shapes=[
            pltpu.VMEM((2, 512, 512), jnp.bfloat16),
            pltpu.VMEM((128, 256), jnp.float32),
            pltpu.VMEM((8, 128, 256), jnp.float32),
            pltpu.VMEM((1024, 128), jnp.float32),
        ],
        input_output_aliases=aliases,
        compiler_params=pltpu.CompilerParams(vmem_limit_bytes=VMEM_LIMIT),
        cost_estimate=pl.CostEstimate(
            flops=count * 4_000_000_000, bytes_accessed=count * 5_000_000, transcendentals=0
        ),
        name="shells_piece",
    )(*operands)


def on_device(pressure, legendre, radial):
    frames, freq_dev, lat_dev, lon_count = pressure.shape
    af_count = lax.axis_size("af")
    sa_count = lax.axis_size("sa")
    pairs_here = legendre.shape[0]
    if (frames, freq_dev, lat_dev, af_count, sa_count) != (4, 8, 128, 4, 8):
        return plain_on_device(pressure, legendre, radial)
    devices = af_count * sa_count
    owner_block = lax.axis_index("af") * sa_count + lax.axis_index("sa")
    base = (owner_block * pairs_here).astype(jnp.int32).reshape(1)
    factors = radial.reshape(LDEG * 32, 128)

    lane = np.arange(256)
    freq = (lane // 32 % 4) * 8 + lane % 8
    rx = (lane // 128) * 4 + lane // 8 % 4
    same = freq[:, None] == lane[None, :] % 32
    pick = np.stack([same & (rx == k)[:, None] for k in range(8)])
    pick = jnp.asarray(pick.astype(jnp.bfloat16))
    flip = jnp.asarray(np.eye(128)[::-1].astype(jnp.bfloat16))

    starts = [sum(CHUNKS[:i]) for i in range(len(CHUNKS))]
    output = None
    waiting = None
    for i, (first, count) in enumerate(zip(starts, CHUNKS)):
        table = jnp.asarray(table_rows(lon_count, devices, pairs_here, first, count))
        spectra = dft(table, pressure)
        if output is not None:
            spectra, output = lax.optimization_barrier((spectra, output))
        spread = spectra.reshape(devices, 4 * count * 32, 128)
        piece = lax.all_to_all(spread, ("af", "sa"), split_axis=0, concat_axis=0, tiled=True)
        piece = piece.reshape(devices, 2, 2, count, 32, 128)
        if waiting is not None:
            output = shells_piece(base, waiting[0], legendre, factors, pick, flip, output, *waiting[1:])
        waiting = (piece, first, count)
    output = shells_piece(base, waiting[0], legendre, factors, pick, flip, output, *waiting[1:])
    return output.reshape(pairs_here, LDEG + 1, 2, frames, 128)


def solution(mesh):
    return jax.shard_map(
        on_device,
        mesh=mesh,
        in_specs=(P(None, "af", "sa", None), P(("af", "sa"), None, None), P()),
        out_specs=P(("af", "sa"), None, None, None, None),
        check_vma=False,
    )
```

```python
import math

import jax
import jax.numpy as jnp
import numpy as np
from jax import lax
from jax.experimental import pallas as pl
from jax.experimental.pallas import tpu as pltpu
from jax.sharding import PartitionSpec as P

LDEG = 1024
CHUNKS = (1, 10, 4, 1)
TILE = 512
VMEM_LIMIT = 62 * 1024 * 1024


def order_of_column(column_count):
    column = lax.iota(jnp.int32, column_count)
    halves = column // 2
    return jnp.where(column % 2 == 0, halves, LDEG - 1 - halves)


def fourier_table(lon_count, orders):
    longitude = lax.iota(jnp.int32, lon_count)
    product = longitude[:, None] * orders[None, :] % lon_count
    phases = product.astype(jnp.float32) * (2.0 * math.pi / lon_count)
    norm_scale = 1.0 / math.sqrt(lon_count)
    return jnp.stack([jnp.cos(phases) * norm_scale, -jnp.sin(phases) * norm_scale], axis=1).astype(
        jnp.bfloat16
    )


def pair_layout(pair_index):
    column = lax.iota(jnp.int32, LDEG + 1)
    segment = (column >= LDEG - pair_index).astype(jnp.int32)
    order_here = jnp.where(segment == 1, LDEG - 1 - pair_index, pair_index)
    degree = jnp.where(segment == 1, column - 1, pair_index + column)
    parity = (degree + order_here) % 2
    return (segment, degree, parity)


def selector(segment, parity):
    branch_ids = lax.iota(jnp.int32, 2)
    seg_match = segment[..., None, None, :] == branch_ids[:, None, None]
    par_match = parity[..., None, None, :] == branch_ids[None, :, None]
    return (seg_match & par_match).astype(jnp.float32)


def harmonics(gathered, legendre, select):
    parts, per_device, frame_count, freqs, lat_count = gathered.shape
    half_count = lat_count // 2
    upper_half = gathered[..., :half_count].astype(jnp.float32)
    lower_half = jnp.flip(gathered[..., half_count:], axis=4).astype(jnp.float32)
    even_part = (upper_half + lower_half).astype(jnp.bfloat16)
    odd_part = (upper_half - lower_half).astype(jnp.bfloat16)
    folded = jnp.stack([even_part, odd_part], axis=2)
    folded = folded.reshape(parts, per_device // 2, 2, 2, frame_count, freqs, half_count)
    products = jnp.einsum(
        "rkstxfj,kqj->krstxfq", folded, legendre, preferred_element_type=jnp.float32
    )
    return jnp.sum(products * select[:, None, :, :, None, None, :], axis=(2, 3)).astype(
        jnp.bfloat16
    )


def plain_on_device(pressure, legendre, radial):
    frames, freq_dev, lat_dev, lon_count = pressure.shape
    af_count = lax.axis_size("af")
    sa_count = lax.axis_size("sa")
    per_device = LDEG // (af_count * sa_count)
    trig_table = fourier_table(lon_count, order_of_column(LDEG))
    spectra = jnp.einsum(
        "krc,xfjk->rcxfj", trig_table, pressure, preferred_element_type=jnp.float32
    ).astype(jnp.bfloat16)
    pairs_here = legendre.shape[0]
    owner_block = lax.axis_index("af") * sa_count + lax.axis_index("sa")
    pair_ids = owner_block * pairs_here + lax.iota(jnp.int32, pairs_here)
    segment, degree, parity = pair_layout(pair_ids[:, None])
    select = selector(segment, parity)
    spread = spectra.reshape(1, 2, af_count * sa_count, per_device, frames, freq_dev, lat_dev)
    piece = lax.all_to_all(spread, ("af", "sa"), split_axis=2, concat_axis=0, tiled=True)
    frame_count = piece.shape[4]
    sources = piece.reshape(af_count, sa_count, 2, per_device, frame_count, freq_dev, lat_dev)
    sources = jnp.transpose(sources, (2, 3, 4, 0, 5, 1, 6))
    gathered = sources.reshape(2, per_device, frame_count, af_count * freq_dev, sa_count * lat_dev)
    harmonic = harmonics(gathered, legendre, select)
    factors = jnp.take(radial, degree.reshape(-1), axis=0)
    factors = factors.reshape(pairs_here, LDEG + 1, radial.shape[1], radial.shape[2])
    result = jnp.einsum("krxfq,kqfs->kqrxs", harmonic, factors, preferred_element_type=jnp.float32)
    return result.astype(jnp.bfloat16)


def table_rows(lon_count, devices, pairs_here, first, count):
    pair = np.arange(devices)[:, None] * pairs_here + first + np.arange(count)[None, :]
    order = np.stack([pair, LDEG - 1 - pair], axis=1)
    product = (order[..., None].astype(np.int64) * np.arange(lon_count)) % lon_count
    phase = product.astype(np.float32) * np.float32(2.0 * math.pi / lon_count)
    scale = np.float32(1.0 / math.sqrt(lon_count))
    rows = np.stack([np.cos(phase) * scale, -np.sin(phase) * scale], axis=1)
    return rows.reshape(devices * 4 * count, lon_count).astype(jnp.bfloat16)


def dot_t(a, b):
    return lax.dot_general(a, b, (((1,), (1,)), ((), ())), preferred_element_type=jnp.float32)


def dft_kernel(table_ref, pressure_ref, out_ref, acc_ref):
    rows = table_ref.shape[0]
    frame = pl.program_id(0)
    for f in range(0, 8, 2):
        block = pressure_ref[0, f : f + 2].reshape(256, pressure_ref.shape[3])
        both = dot_t(table_ref[...], block)
        at = (frame % 2) * 8 + f
        acc_ref[pl.ds(at, rows, stride=16), :] = both[:, :128]
        acc_ref[pl.ds(at + 1, rows, stride=16), :] = both[:, 128:]

    @pl.when(frame % 2 == 1)
    def _():
        out_ref[...] = acc_ref[...].reshape(rows, 16, 128).astype(jnp.bfloat16)


def dft(table, pressure):
    rows, lon_count = table.shape
    return pl.pallas_call(
        dft_kernel,
        grid=(4,),
        in_specs=[
            pl.BlockSpec((rows, lon_count), lambda x: (0, 0), pipeline_mode=pl.Buffered(1)),
            pl.BlockSpec((1, 8, 128, lon_count), lambda x: (x, 0, 0, 0)),
        ],
        out_specs=pl.BlockSpec((rows, 16, 128), lambda x: (0, x // 2, 0)),
        out_shape=jax.ShapeDtypeStruct((rows, 32, 128), jnp.bfloat16),
        scratch_shapes=[pltpu.VMEM((rows * 16, 128), jnp.float32)],
        compiler_params=pltpu.CompilerParams(vmem_limit_bytes=VMEM_LIMIT),
        cost_estimate=pl.CostEstimate(
            flops=2 * rows * 4096 * lon_count, bytes_accessed=1 << 24, transcendentals=0
        ),
        name="dft_piece",
    )(table, pressure)


def shells_kernel(first, *refs):
    base_ref, recv_ref, leg_ref, rad_ref, pick_ref, turn_ref = refs[:6]
    out_ref, both_ref, harm_ref, copies_ref, result_ref = refs[-5:]
    pair = base_ref[0] + first + pl.program_id(0)
    bound = LDEG - pair

    for s in range(4):
        for seg in range(2):
            for half, sa in ((0, s), (1, 7 - s)):
                rows = [recv_ref[8 * a + sa, r, seg, 0] for r in range(2) for a in range(4)]
                turned = dot_t(turn_ref[half], jnp.concatenate(rows, axis=0))
                lanes = slice(256 * half, 256 * half + 256)
                both_ref[seg, 128 * s : 128 * s + 128, lanes] = turned.astype(jnp.bfloat16)

    own_q = (
        lax.broadcasted_iota(jnp.int32, (64, 256), 1) // 32
        == lax.broadcasted_iota(jnp.int32, (64, 256), 0) % 8
    )

    def legendre_rows(rows, start, seg):
        product = jnp.dot(rows, both_ref[seg], preferred_element_type=jnp.float32)
        q = start + lax.broadcasted_iota(jnp.int32, (rows.shape[0], 256), 0)
        parity = (q + seg * pair) % 2
        north, south = product[:, :256], product[:, 256:]
        return q, north + jnp.where(parity == 0, south, -south)

    def degree(q):
        return jnp.where(q >= bound, q - 1, pair + q)

    def factors_at(degree_here):
        return rad_ref[pl.ds(pl.multiple_of(degree_here * 32, 32), 32), :]

    def fill_copies(harm):
        harm = harm.astype(jnp.bfloat16)
        for rx in range(8):
            copies_ref[rx, 0 : harm.shape[0]] = jnp.dot(
                harm, pick_ref[rx], preferred_element_type=jnp.float32
            )

    def radial_block(block, slab):
        rows = [copies_ref[rx, 8 * block : 8 * block + 8] for rx in range(8)]
        diagonal = jnp.where(own_q, jnp.concatenate(rows, axis=0), 0.0).astype(jnp.bfloat16)
        result = jnp.dot(diagonal, slab, preferred_element_type=jnp.float32)
        for rx in range(8):
            result_ref[pl.ds(64 * block + rx, 8, stride=8), :] = result[8 * rx : 8 * rx + 8]

    def columns(start, rows, slabs):
        count = rows.shape[0]

        @pl.when(start < bound)
        def _():
            _, harm = legendre_rows(rows, start, 0)
            harm_ref[0:count] = harm

        @pl.when(start + count > bound)
        def _():
            q, harm = legendre_rows(rows, start, 1)
            harm_ref[0:count] = jnp.where(q >= bound, harm, harm_ref[0:count])

        fill_copies(harm_ref[0:count])
        for block, slab in enumerate(slabs):
            radial_block(block, jnp.concatenate(slab(), axis=0))
        at = pl.multiple_of(start * 8, 1024)
        out_rows = min(8 * count, 8 * (LDEG + 1) - 8 * (LDEG - TILE))
        out_ref[0, pl.ds(at, out_rows), :] = result_ref[0:out_rows].astype(jnp.bfloat16)

    def slab_of(start, block):
        return lambda: [factors_at(degree(start + 8 * block + k)) for k in range(8)]

    @pl.loop(0, LDEG // TILE - 1)
    def _(tile):
        start = pl.multiple_of(tile * TILE, TILE)
        rows = leg_ref[0, pl.ds(start, TILE), :]
        columns(start, rows, [slab_of(start, block) for block in range(TILE // 8)])

    start = LDEG - TILE
    last = leg_ref[0, LDEG : LDEG + 1, :].astype(jnp.float32)
    last = jnp.broadcast_to(last, (16, 512)).astype(jnp.bfloat16)
    rows = jnp.concatenate([leg_ref[0, start:LDEG, :], last], axis=0)
    slabs = [slab_of(start, block) for block in range(TILE // 8)]
    slabs.append(lambda: [factors_at(LDEG - 1)] * 8)
    columns(start, rows, slabs)


def shells_piece(base, received, legendre, radial, pick, turn, output, first, count):
    pairs_here = legendre.shape[0]
    rows = 8 * (LDEG + 1)
    once = pl.Buffered(1)
    in_specs = [
        pl.BlockSpec(memory_space=pltpu.SMEM),
        pl.BlockSpec((32, 2, 2, 1, 32, 128), lambda i: (0, 0, 0, i, 0, 0)),
        pl.BlockSpec((1, LDEG + 1, 512), lambda i: (first + i, 0, 0)),
        pl.BlockSpec(radial.shape, lambda i: (0, 0), pipeline_mode=once),
        pl.BlockSpec((8, 256, 256), lambda i: (0, 0, 0)),
        pl.BlockSpec((2, 128, 128), lambda i: (0, 0, 0)),
    ]
    operands = [base, received, legendre, radial, pick, turn]
    aliases = {}
    if output is not None:
        in_specs.append(pl.BlockSpec(memory_space=pl.ANY))
        operands.append(output)
        aliases = {6: 0}

    def kernel(*refs):
        shells_kernel(first, *refs)

    return pl.pallas_call(
        kernel,
        grid=(count,),
        in_specs=in_specs,
        out_specs=pl.BlockSpec((1, rows, 128), lambda i: (first + i, 0, 0)),
        out_shape=jax.ShapeDtypeStruct((pairs_here, rows, 128), jnp.bfloat16),
        scratch_shapes=[
            pltpu.VMEM((2, 512, 512), jnp.bfloat16),
            pltpu.VMEM((TILE + 16, 256), jnp.float32),
            pltpu.VMEM((8, TILE + 16, 256), jnp.float32),
            pltpu.VMEM((8 * TILE + 128, 128), jnp.float32),
        ],
        input_output_aliases=aliases,
        compiler_params=pltpu.CompilerParams(vmem_limit_bytes=VMEM_LIMIT),
        cost_estimate=pl.CostEstimate(
            flops=count * 4_000_000_000, bytes_accessed=count * 5_000_000, transcendentals=0
        ),
        name="shells_piece",
    )(*operands)


def on_device(pressure, legendre, radial):
    frames, freq_dev, lat_dev, lon_count = pressure.shape
    af_count = lax.axis_size("af")
    sa_count = lax.axis_size("sa")
    pairs_here = legendre.shape[0]
    if (frames, freq_dev, lat_dev, af_count, sa_count) != (4, 8, 128, 4, 8):
        return plain_on_device(pressure, legendre, radial)
    devices = af_count * sa_count
    owner_block = lax.axis_index("af") * sa_count + lax.axis_index("sa")
    base = (owner_block * pairs_here).astype(jnp.int32).reshape(1)
    factors = radial.reshape(LDEG * 32, 128)

    lane = np.arange(256)
    freq = (lane // 32 % 4) * 8 + lane % 8
    rx = (lane // 128) * 4 + lane // 8 % 4
    same = freq[:, None] == lane[None, :] % 32
    pick = np.stack([same & (rx == k)[:, None] for k in range(8)])
    pick = jnp.asarray(pick.astype(jnp.bfloat16))
    turn = jnp.asarray(np.stack([np.eye(128), np.eye(128)[::-1]]).astype(jnp.bfloat16))

    starts = [sum(CHUNKS[:i]) for i in range(len(CHUNKS))]
    output = None
    waiting = None
    for i, (first, count) in enumerate(zip(starts, CHUNKS)):
        table = jnp.asarray(table_rows(lon_count, devices, pairs_here, first, count))
        spectra = dft(table, pressure)
        if output is not None:
            spectra, output = lax.optimization_barrier((spectra, output))
        spread = spectra.reshape(devices, 4 * count * 32, 128)
        piece = lax.all_to_all(spread, ("af", "sa"), split_axis=0, concat_axis=0, tiled=True)
        piece = piece.reshape(devices, 2, 2, count, 32, 128)
        if waiting is not None:
            output = shells_piece(base, waiting[0], legendre, factors, pick, turn, output, *waiting[1:])
        waiting = (piece, first, count)
    output = shells_piece(base, waiting[0], legendre, factors, pick, turn, output, *waiting[1:])
    return output.reshape(pairs_here, LDEG + 1, 2, frames, 128)


def solution(mesh):
    return jax.shard_map(
        on_device,
        mesh=mesh,
        in_specs=(P(None, "af", "sa", None), P(("af", "sa"), None, None), P()),
        out_specs=P(("af", "sa"), None, None, None, None),
        check_vma=False,
    )
```

```python
import math

import jax
import jax.numpy as jnp
import numpy as np
from jax import lax
from jax.experimental import pallas as pl
from jax.experimental.pallas import tpu as pltpu
from jax.sharding import PartitionSpec as P

LDEG = 1024
CHUNKS = (2, 10, 3, 1)
TILE = 512
VMEM_LIMIT = 63 * 1024 * 1024


def order_of_column(column_count):
    column = lax.iota(jnp.int32, column_count)
    halves = column // 2
    return jnp.where(column % 2 == 0, halves, LDEG - 1 - halves)


def fourier_table(lon_count, orders):
    longitude = lax.iota(jnp.int32, lon_count)
    product = longitude[:, None] * orders[None, :] % lon_count
    phases = product.astype(jnp.float32) * (2.0 * math.pi / lon_count)
    norm_scale = 1.0 / math.sqrt(lon_count)
    return jnp.stack([jnp.cos(phases) * norm_scale, -jnp.sin(phases) * norm_scale], axis=1).astype(
        jnp.bfloat16
    )


def pair_layout(pair_index):
    column = lax.iota(jnp.int32, LDEG + 1)
    segment = (column >= LDEG - pair_index).astype(jnp.int32)
    order_here = jnp.where(segment == 1, LDEG - 1 - pair_index, pair_index)
    degree = jnp.where(segment == 1, column - 1, pair_index + column)
    parity = (degree + order_here) % 2
    return (segment, degree, parity)


def selector(segment, parity):
    branch_ids = lax.iota(jnp.int32, 2)
    seg_match = segment[..., None, None, :] == branch_ids[:, None, None]
    par_match = parity[..., None, None, :] == branch_ids[None, :, None]
    return (seg_match & par_match).astype(jnp.float32)


def harmonics(gathered, legendre, select):
    parts, per_device, frame_count, freqs, lat_count = gathered.shape
    half_count = lat_count // 2
    upper_half = gathered[..., :half_count].astype(jnp.float32)
    lower_half = jnp.flip(gathered[..., half_count:], axis=4).astype(jnp.float32)
    even_part = (upper_half + lower_half).astype(jnp.bfloat16)
    odd_part = (upper_half - lower_half).astype(jnp.bfloat16)
    folded = jnp.stack([even_part, odd_part], axis=2)
    folded = folded.reshape(parts, per_device // 2, 2, 2, frame_count, freqs, half_count)
    products = jnp.einsum(
        "rkstxfj,kqj->krstxfq", folded, legendre, preferred_element_type=jnp.float32
    )
    return jnp.sum(products * select[:, None, :, :, None, None, :], axis=(2, 3)).astype(
        jnp.bfloat16
    )


def plain_on_device(pressure, legendre, radial):
    frames, freq_dev, lat_dev, lon_count = pressure.shape
    af_count = lax.axis_size("af")
    sa_count = lax.axis_size("sa")
    per_device = LDEG // (af_count * sa_count)
    trig_table = fourier_table(lon_count, order_of_column(LDEG))
    spectra = jnp.einsum(
        "krc,xfjk->rcxfj", trig_table, pressure, preferred_element_type=jnp.float32
    ).astype(jnp.bfloat16)
    pairs_here = legendre.shape[0]
    owner_block = lax.axis_index("af") * sa_count + lax.axis_index("sa")
    pair_ids = owner_block * pairs_here + lax.iota(jnp.int32, pairs_here)
    segment, degree, parity = pair_layout(pair_ids[:, None])
    select = selector(segment, parity)
    spread = spectra.reshape(1, 2, af_count * sa_count, per_device, frames, freq_dev, lat_dev)
    piece = lax.all_to_all(spread, ("af", "sa"), split_axis=2, concat_axis=0, tiled=True)
    frame_count = piece.shape[4]
    sources = piece.reshape(af_count, sa_count, 2, per_device, frame_count, freq_dev, lat_dev)
    sources = jnp.transpose(sources, (2, 3, 4, 0, 5, 1, 6))
    gathered = sources.reshape(2, per_device, frame_count, af_count * freq_dev, sa_count * lat_dev)
    harmonic = harmonics(gathered, legendre, select)
    factors = jnp.take(radial, degree.reshape(-1), axis=0)
    factors = factors.reshape(pairs_here, LDEG + 1, radial.shape[1], radial.shape[2])
    result = jnp.einsum("krxfq,kqfs->kqrxs", harmonic, factors, preferred_element_type=jnp.float32)
    return result.astype(jnp.bfloat16)


def table_rows(lon_count, devices, pairs_here, first, count):
    pair = np.arange(devices)[:, None] * pairs_here + first + np.arange(count)[None, :]
    order = np.stack([pair, LDEG - 1 - pair], axis=1)
    product = (order[..., None].astype(np.int64) * np.arange(lon_count)) % lon_count
    phase = product.astype(np.float32) * np.float32(2.0 * math.pi / lon_count)
    scale = np.float32(1.0 / math.sqrt(lon_count))
    rows = np.stack([np.cos(phase) * scale, -np.sin(phase) * scale], axis=1)
    return rows.reshape(devices * 4 * count, lon_count).astype(jnp.bfloat16)


def dot_t(a, b):
    return lax.dot_general(a, b, (((1,), (1,)), ((), ())), preferred_element_type=jnp.float32)


def dft_kernel(table_ref, pressure_ref, out_ref, acc_ref):
    rows = table_ref.shape[0]
    frame = pl.program_id(0)
    for f in range(0, 8, 2):
        block = pressure_ref[0, f : f + 2].reshape(256, pressure_ref.shape[3])
        both = dot_t(table_ref[...], block)
        at = (frame % 2) * 8 + f
        acc_ref[pl.ds(at, rows, stride=16), :] = both[:, :128]
        acc_ref[pl.ds(at + 1, rows, stride=16), :] = both[:, 128:]

    @pl.when(frame % 2 == 1)
    def _():
        out_ref[...] = acc_ref[...].reshape(rows, 16, 128).astype(jnp.bfloat16)


def dft(table, pressure):
    rows, lon_count = table.shape
    return pl.pallas_call(
        dft_kernel,
        grid=(4,),
        in_specs=[
            pl.BlockSpec((rows, lon_count), lambda x: (0, 0), pipeline_mode=pl.Buffered(1)),
            pl.BlockSpec((1, 8, 128, lon_count), lambda x: (x, 0, 0, 0)),
        ],
        out_specs=pl.BlockSpec((rows, 16, 128), lambda x: (0, x // 2, 0)),
        out_shape=jax.ShapeDtypeStruct((rows, 32, 128), jnp.bfloat16),
        scratch_shapes=[pltpu.VMEM((rows * 16, 128), jnp.float32)],
        compiler_params=pltpu.CompilerParams(vmem_limit_bytes=VMEM_LIMIT),
        cost_estimate=pl.CostEstimate(
            flops=2 * rows * 4096 * lon_count, bytes_accessed=1 << 24, transcendentals=0
        ),
        name="dft_piece",
    )(table, pressure)


def shells_kernel(first, *refs):
    base_ref, recv_ref, leg_ref, rad_hbm_ref, pick_ref, turn_ref = refs[:6]
    out_ref, both_ref, harm_ref, copies_ref, result_ref, rad_ref, rad_sem = refs[-7:]
    pair = base_ref[0] + first + pl.program_id(0)
    bound = LDEG - pair
    quarter = rad_ref.shape[0] // 4
    radial_copies = [
        pltpu.make_async_copy(
            rad_hbm_ref.at[pl.ds(k * quarter, quarter)],
            rad_ref.at[pl.ds(k * quarter, quarter)],
            rad_sem.at[k],
        )
        for k in range(4)
    ]

    @pl.when(pl.program_id(0) == 0)
    def _():
        for copy in radial_copies:
            copy.start()

    for s in range(4):
        for seg in range(2):
            for half, sa in ((0, s), (1, 7 - s)):
                rows = [recv_ref[8 * a + sa, r, seg, 0] for r in range(2) for a in range(4)]
                turned = dot_t(turn_ref[half], jnp.concatenate(rows, axis=0))
                lanes = slice(256 * half, 256 * half + 256)
                both_ref[seg, 128 * s : 128 * s + 128, lanes] = turned.astype(jnp.bfloat16)

    own_q = (
        lax.broadcasted_iota(jnp.int32, (1, 8, 256), 2) // 32
        == lax.broadcasted_iota(jnp.int32, (1, 8, 256), 1)
    )

    def legendre_rows(rows, start, seg):
        product = jnp.dot(rows, both_ref[seg], preferred_element_type=jnp.float32)
        q = start + lax.broadcasted_iota(jnp.int32, (rows.shape[0], 256), 0)
        parity = (q + seg * pair) % 2
        north, south = product[:, :256], product[:, 256:]
        return q, north + jnp.where(parity == 0, south, -south)

    def degree(q):
        return jnp.where(q >= bound, q - 1, pair + q)

    def factors_at(degree_here):
        return rad_ref[pl.ds(pl.multiple_of(degree_here * 32, 32), 32), :]

    def fill_copies(harm):
        count = harm.shape[0]
        harm = harm.astype(jnp.bfloat16)
        for rx in range(8):
            copies = jnp.dot(harm, pick_ref[rx], preferred_element_type=jnp.float32)
            own = jnp.where(own_q, copies.reshape(count // 8, 8, 256), 0.0)
            copies_ref[rx, 0:count] = own.reshape(count, 256).astype(jnp.bfloat16)

    def radial_block(block, slab):
        rows = [copies_ref[rx, 16 * block : 16 * block + 16] for rx in range(8)]
        rows = jnp.concatenate(rows, axis=0)
        result = jnp.dot(rows, slab, preferred_element_type=jnp.float32)
        for rx in range(8):
            for half in range(2):
                at = 128 * block + 64 * half + rx
                part = result[16 * rx + 8 * half :, 128 * half : 128 * half + 128]
                result_ref[pl.ds(at, 8, stride=8), :] = part[:8]

    def columns(start, rows, slabs, first_tile):
        count = rows.shape[0]

        @pl.when(start < bound)
        def _():
            _, harm = legendre_rows(rows, start, 0)
            harm_ref[0:count] = harm

        @pl.when(start + count > bound)
        def _():
            q, harm = legendre_rows(rows, start, 1)
            harm_ref[0:count] = jnp.where(q >= bound, harm, harm_ref[0:count])

        fill_copies(harm_ref[0:count])
        if first_tile:

            @pl.when(pl.program_id(0) == 0)
            def _():
                for copy in radial_copies:
                    copy.wait()

        for block, slab in enumerate(slabs):
            radial_block(block, slab())
        out_rows = min(8 * count, 8 * (LDEG + 1) - 8 * (LDEG - TILE))
        out_ref[0, 8 * start : 8 * start + out_rows, :] = result_ref[0:out_rows].astype(jnp.bfloat16)

    def slab_of(start, block):
        def slab():
            q = start + 16 * block
            halves = [[factors_at(degree(q + 8 * half + k)) for k in range(8)] for half in range(2)]
            return jnp.concatenate([jnp.concatenate(h, axis=0) for h in halves], axis=1)

        return slab

    for start in range(0, LDEG - TILE, TILE):
        rows = leg_ref[0, start : start + TILE, :]
        columns(start, rows, [slab_of(start, block) for block in range(TILE // 16)], start == 0)

    start = LDEG - TILE
    last = leg_ref[0, LDEG : LDEG + 1, :].astype(jnp.float32)
    last = jnp.broadcast_to(last, (16, 512)).astype(jnp.bfloat16)
    rows = jnp.concatenate([leg_ref[0, start:LDEG, :], last], axis=0)
    slabs = [slab_of(start, block) for block in range(TILE // 16)]
    slabs.append(lambda: jnp.tile(factors_at(LDEG - 1), (8, 2)))
    columns(start, rows, slabs, False)


def shells_piece(base, received, legendre, radial, pick, turn, output, first, count):
    pairs_here = legendre.shape[0]
    rows = 8 * (LDEG + 1)
    in_specs = [
        pl.BlockSpec(memory_space=pltpu.SMEM),
        pl.BlockSpec((32, 2, 2, 1, 32, 128), lambda i: (0, 0, 0, i, 0, 0)),
        pl.BlockSpec((1, LDEG + 1, 512), lambda i: (first + i, 0, 0)),
        pl.BlockSpec(memory_space=pl.ANY),
        pl.BlockSpec((8, 256, 256), lambda i: (0, 0, 0)),
        pl.BlockSpec((2, 128, 128), lambda i: (0, 0, 0)),
    ]
    operands = [base, received, legendre, radial, pick, turn]
    aliases = {}
    if output is not None:
        in_specs.append(pl.BlockSpec(memory_space=pl.ANY))
        operands.append(output)
        aliases = {6: 0}

    def kernel(*refs):
        shells_kernel(first, *refs)

    return pl.pallas_call(
        kernel,
        grid=(count,),
        in_specs=in_specs,
        out_specs=pl.BlockSpec((1, rows, 128), lambda i: (first + i, 0, 0)),
        out_shape=jax.ShapeDtypeStruct((pairs_here, rows, 128), jnp.bfloat16),
        scratch_shapes=[
            pltpu.VMEM((2, 512, 512), jnp.bfloat16),
            pltpu.VMEM((TILE + 16, 256), jnp.float32),
            pltpu.VMEM((8, TILE + 16, 256), jnp.bfloat16),
            pltpu.VMEM((8 * TILE + 128, 128), jnp.float32),
            pltpu.VMEM(radial.shape, jnp.bfloat16),
            pltpu.SemaphoreType.DMA((4,)),
        ],
        input_output_aliases=aliases,
        compiler_params=pltpu.CompilerParams(vmem_limit_bytes=VMEM_LIMIT),
        cost_estimate=pl.CostEstimate(
            flops=count * 4_000_000_000, bytes_accessed=count * 5_000_000, transcendentals=0
        ),
        name="shells_piece",
    )(*operands)


def on_device(pressure, legendre, radial):
    frames, freq_dev, lat_dev, lon_count = pressure.shape
    af_count = lax.axis_size("af")
    sa_count = lax.axis_size("sa")
    pairs_here = legendre.shape[0]
    if (frames, freq_dev, lat_dev, af_count, sa_count) != (4, 8, 128, 4, 8):
        return plain_on_device(pressure, legendre, radial)
    devices = af_count * sa_count
    owner_block = lax.axis_index("af") * sa_count + lax.axis_index("sa")
    base = (owner_block * pairs_here).astype(jnp.int32).reshape(1)
    factors = radial.reshape(LDEG * 32, 128)

    lane = np.arange(256)
    freq = (lane // 32 % 4) * 8 + lane % 8
    rx = (lane // 128) * 4 + lane // 8 % 4
    same = freq[:, None] == lane[None, :] % 32
    pick = np.stack([same & (rx == k)[:, None] for k in range(8)])
    pick = jnp.asarray(pick.astype(jnp.bfloat16))
    turn = jnp.asarray(np.stack([np.eye(128), np.eye(128)[::-1]]).astype(jnp.bfloat16))

    starts = [sum(CHUNKS[:i]) for i in range(len(CHUNKS))]
    tables = [
        jnp.asarray(table_rows(lon_count, devices, pairs_here, first, count))
        for first, count in zip(starts, CHUNKS)
    ]
    spectra = [dft(table, pressure) for table in tables]
    output = None
    waiting = None
    for i, (first, count) in enumerate(zip(starts, CHUNKS)):
        if output is not None:
            spectra[i], output = lax.optimization_barrier((spectra[i], output))
        if i == len(CHUNKS) - 2:
            spectra[i:] = lax.optimization_barrier(tuple(spectra[i:]))
        spread = spectra[i].reshape(devices, 4 * count * 32, 128)
        piece = lax.all_to_all(spread, ("af", "sa"), split_axis=0, concat_axis=0, tiled=True)
        piece = piece.reshape(devices, 2, 2, count, 32, 128)
        if waiting is not None:
            output = shells_piece(base, waiting[0], legendre, factors, pick, turn, output, *waiting[1:])
        waiting = (piece, first, count)
    output = shells_piece(base, waiting[0], legendre, factors, pick, turn, output, *waiting[1:])
    return output.reshape(pairs_here, LDEG + 1, 2, frames, 128)


def solution(mesh):
    return jax.shard_map(
        on_device,
        mesh=mesh,
        in_specs=(P(None, "af", "sa", None), P(("af", "sa"), None, None), P()),
        out_specs=P(("af", "sa"), None, None, None, None),
        check_vma=False,
    )
```

```python
import math

import jax
import jax.numpy as jnp
import numpy as np
from jax import lax
from jax.experimental import pallas as pl
from jax.experimental.pallas import tpu as pltpu
from jax.sharding import PartitionSpec as P

LDEG = 1024
CHUNKS = (2, 10, 3, 1)
TILE = 1024
VMEM_LIMIT = 63 * 1024 * 1024


def order_of_column(column_count):
    column = lax.iota(jnp.int32, column_count)
    halves = column // 2
    return jnp.where(column % 2 == 0, halves, LDEG - 1 - halves)


def fourier_table(lon_count, orders):
    longitude = lax.iota(jnp.int32, lon_count)
    product = longitude[:, None] * orders[None, :] % lon_count
    phases = product.astype(jnp.float32) * (2.0 * math.pi / lon_count)
    norm_scale = 1.0 / math.sqrt(lon_count)
    return jnp.stack([jnp.cos(phases) * norm_scale, -jnp.sin(phases) * norm_scale], axis=1).astype(
        jnp.bfloat16
    )


def pair_layout(pair_index):
    column = lax.iota(jnp.int32, LDEG + 1)
    segment = (column >= LDEG - pair_index).astype(jnp.int32)
    order_here = jnp.where(segment == 1, LDEG - 1 - pair_index, pair_index)
    degree = jnp.where(segment == 1, column - 1, pair_index + column)
    parity = (degree + order_here) % 2
    return (segment, degree, parity)


def selector(segment, parity):
    branch_ids = lax.iota(jnp.int32, 2)
    seg_match = segment[..., None, None, :] == branch_ids[:, None, None]
    par_match = parity[..., None, None, :] == branch_ids[None, :, None]
    return (seg_match & par_match).astype(jnp.float32)


def harmonics(gathered, legendre, select):
    parts, per_device, frame_count, freqs, lat_count = gathered.shape
    half_count = lat_count // 2
    upper_half = gathered[..., :half_count].astype(jnp.float32)
    lower_half = jnp.flip(gathered[..., half_count:], axis=4).astype(jnp.float32)
    even_part = (upper_half + lower_half).astype(jnp.bfloat16)
    odd_part = (upper_half - lower_half).astype(jnp.bfloat16)
    folded = jnp.stack([even_part, odd_part], axis=2)
    folded = folded.reshape(parts, per_device // 2, 2, 2, frame_count, freqs, half_count)
    products = jnp.einsum(
        "rkstxfj,kqj->krstxfq", folded, legendre, preferred_element_type=jnp.float32
    )
    return jnp.sum(products * select[:, None, :, :, None, None, :], axis=(2, 3)).astype(
        jnp.bfloat16
    )


def plain_on_device(pressure, legendre, radial):
    frames, freq_dev, lat_dev, lon_count = pressure.shape
    af_count = lax.axis_size("af")
    sa_count = lax.axis_size("sa")
    per_device = LDEG // (af_count * sa_count)
    trig_table = fourier_table(lon_count, order_of_column(LDEG))
    spectra = jnp.einsum(
        "krc,xfjk->rcxfj", trig_table, pressure, preferred_element_type=jnp.float32
    ).astype(jnp.bfloat16)
    pairs_here = legendre.shape[0]
    owner_block = lax.axis_index("af") * sa_count + lax.axis_index("sa")
    pair_ids = owner_block * pairs_here + lax.iota(jnp.int32, pairs_here)
    segment, degree, parity = pair_layout(pair_ids[:, None])
    select = selector(segment, parity)
    spread = spectra.reshape(1, 2, af_count * sa_count, per_device, frames, freq_dev, lat_dev)
    piece = lax.all_to_all(spread, ("af", "sa"), split_axis=2, concat_axis=0, tiled=True)
    frame_count = piece.shape[4]
    sources = piece.reshape(af_count, sa_count, 2, per_device, frame_count, freq_dev, lat_dev)
    sources = jnp.transpose(sources, (2, 3, 4, 0, 5, 1, 6))
    gathered = sources.reshape(2, per_device, frame_count, af_count * freq_dev, sa_count * lat_dev)
    harmonic = harmonics(gathered, legendre, select)
    factors = jnp.take(radial, degree.reshape(-1), axis=0)
    factors = factors.reshape(pairs_here, LDEG + 1, radial.shape[1], radial.shape[2])
    result = jnp.einsum("krxfq,kqfs->kqrxs", harmonic, factors, preferred_element_type=jnp.float32)
    return result.astype(jnp.bfloat16)


def table_rows(lon_count, devices, pairs_here, first, count):
    pair = np.arange(devices)[:, None] * pairs_here + first + np.arange(count)[None, :]
    order = np.stack([pair, LDEG - 1 - pair], axis=1)
    product = (order[..., None].astype(np.int64) * np.arange(lon_count)) % lon_count
    phase = product.astype(np.float32) * np.float32(2.0 * math.pi / lon_count)
    scale = np.float32(1.0 / math.sqrt(lon_count))
    rows = np.stack([np.cos(phase) * scale, -np.sin(phase) * scale], axis=1)
    return rows.reshape(devices * 4 * count, lon_count).astype(jnp.bfloat16)


def dot_t(a, b):
    return lax.dot_general(a, b, (((1,), (1,)), ((), ())), preferred_element_type=jnp.float32)


def dft_kernel(table_ref, pressure_ref, out_ref, acc_ref):
    rows = table_ref.shape[0]
    frame = pl.program_id(0)
    for f in range(0, 8, 2):
        block = pressure_ref[0, f : f + 2].reshape(256, pressure_ref.shape[3])
        both = dot_t(table_ref[...], block)
        at = (frame % 2) * 8 + f
        acc_ref[pl.ds(at, rows, stride=16), :] = both[:, :128]
        acc_ref[pl.ds(at + 1, rows, stride=16), :] = both[:, 128:]

    @pl.when(frame % 2 == 1)
    def _():
        out_ref[...] = acc_ref[...].reshape(rows, 16, 128).astype(jnp.bfloat16)


def dft(table, pressure):
    rows, lon_count = table.shape
    return pl.pallas_call(
        dft_kernel,
        grid=(4,),
        in_specs=[
            pl.BlockSpec((rows, lon_count), lambda x: (0, 0), pipeline_mode=pl.Buffered(1)),
            pl.BlockSpec((1, 8, 128, lon_count), lambda x: (x, 0, 0, 0)),
        ],
        out_specs=pl.BlockSpec((rows, 16, 128), lambda x: (0, x // 2, 0)),
        out_shape=jax.ShapeDtypeStruct((rows, 32, 128), jnp.bfloat16),
        scratch_shapes=[pltpu.VMEM((rows * 16, 128), jnp.float32)],
        compiler_params=pltpu.CompilerParams(vmem_limit_bytes=VMEM_LIMIT),
        cost_estimate=pl.CostEstimate(
            flops=2 * rows * 4096 * lon_count, bytes_accessed=1 << 24, transcendentals=0
        ),
        name="dft_piece",
    )(table, pressure)


def shells_kernel(first, *refs):
    base_ref, recv_ref, leg_ref, rad_hbm_ref, pick_ref, turn_ref = refs[:6]
    out_ref, both_ref, harm_ref, copies_ref, result_ref, rad_ref, rad_sem = refs[-7:]
    pair = base_ref[0] + first + pl.program_id(0)
    bound = LDEG - pair
    quarter = rad_ref.shape[0] // 4
    radial_copies = [
        pltpu.make_async_copy(
            rad_hbm_ref.at[pl.ds(k * quarter, quarter)],
            rad_ref.at[pl.ds(k * quarter, quarter)],
            rad_sem.at[k],
        )
        for k in range(4)
    ]

    @pl.when(pl.program_id(0) == 0)
    def _():
        for copy in radial_copies:
            copy.start()

    for s in range(4):
        for seg in range(2):
            for half, sa in ((0, s), (1, 7 - s)):
                rows = [recv_ref[8 * a + sa, r, seg, 0] for r in range(2) for a in range(4)]
                turned = dot_t(turn_ref[half], jnp.concatenate(rows, axis=0))
                lanes = slice(256 * half, 256 * half + 256)
                both_ref[seg, 128 * s : 128 * s + 128, lanes] = turned.astype(jnp.bfloat16)

    own_q = (
        lax.broadcasted_iota(jnp.int32, (1, 8, 256), 2) // 32
        == lax.broadcasted_iota(jnp.int32, (1, 8, 256), 1)
    )

    def legendre_rows(rows, start, seg):
        product = jnp.dot(rows, both_ref[seg], preferred_element_type=jnp.float32)
        q = start + lax.broadcasted_iota(jnp.int32, (rows.shape[0], 256), 0)
        parity = (q + seg * pair) % 2
        north, south = product[:, :256], product[:, 256:]
        return q, north + jnp.where(parity == 0, south, -south)

    def degree(q):
        return jnp.where(q >= bound, q - 1, pair + q)

    def factors_at(degree_here):
        return rad_ref[pl.ds(pl.multiple_of(degree_here * 32, 32), 32), :]

    def fill_copies(harm):
        count = harm.shape[0]
        harm = harm.astype(jnp.bfloat16)
        for rx in range(8):
            copies = jnp.dot(harm, pick_ref[rx], preferred_element_type=jnp.float32)
            own = jnp.where(own_q, copies.reshape(count // 8, 8, 256), 0.0)
            copies_ref[rx, 0:count] = own.reshape(count, 256).astype(jnp.bfloat16)

    def radial_block(block, slab):
        rows = [copies_ref[rx, 16 * block : 16 * block + 16] for rx in range(8)]
        rows = jnp.concatenate(rows, axis=0)
        result = jnp.dot(rows, slab, preferred_element_type=jnp.float32)
        for rx in range(8):
            for half in range(2):
                at = 128 * block + 64 * half + rx
                part = result[16 * rx + 8 * half :, 128 * half : 128 * half + 128]
                result_ref[pl.ds(at, 8, stride=8), :] = part[:8]

    def columns(start, rows, slabs, first_tile):
        count = rows.shape[0]

        @pl.when(start < bound)
        def _():
            _, harm = legendre_rows(rows, start, 0)
            harm_ref[0:count] = harm

        @pl.when(start + count > bound)
        def _():
            q, harm = legendre_rows(rows, start, 1)
            harm_ref[0:count] = jnp.where(q >= bound, harm, harm_ref[0:count])

        fill_copies(harm_ref[0:count])
        if first_tile:

            @pl.when(pl.program_id(0) == 0)
            def _():
                for copy in radial_copies:
                    copy.wait()

        for block, slab in enumerate(slabs):
            radial_block(block, slab())
        out_rows = min(8 * count, 8 * (LDEG + 1) - 8 * (LDEG - TILE))
        out_ref[0, 8 * start : 8 * start + out_rows, :] = result_ref[0:out_rows].astype(jnp.bfloat16)

    def slab_of(start, block):
        def slab():
            q = start + 16 * block
            halves = [[factors_at(degree(q + 8 * half + k)) for k in range(8)] for half in range(2)]
            return jnp.concatenate([jnp.concatenate(h, axis=0) for h in halves], axis=1)

        return slab

    for start in range(0, LDEG - TILE, TILE):
        rows = leg_ref[0, start : start + TILE, :]
        columns(start, rows, [slab_of(start, block) for block in range(TILE // 16)], start == 0)

    start = LDEG - TILE
    last = leg_ref[0, LDEG : LDEG + 1, :].astype(jnp.float32)
    last = jnp.broadcast_to(last, (16, 512)).astype(jnp.bfloat16)
    rows = jnp.concatenate([leg_ref[0, start:LDEG, :], last], axis=0)
    slabs = [slab_of(start, block) for block in range(TILE // 16)]
    slabs.append(lambda: jnp.tile(factors_at(LDEG - 1), (8, 2)))
    columns(start, rows, slabs, start == 0)


def shells_piece(base, received, legendre, radial, pick, turn, output, first, count):
    pairs_here = legendre.shape[0]
    rows = 8 * (LDEG + 1)
    in_specs = [
        pl.BlockSpec(memory_space=pltpu.SMEM),
        pl.BlockSpec((32, 2, 2, 1, 32, 128), lambda i: (0, 0, 0, i, 0, 0)),
        pl.BlockSpec((1, LDEG + 1, 512), lambda i: (first + i, 0, 0)),
        pl.BlockSpec(memory_space=pl.ANY),
        pl.BlockSpec((8, 256, 256), lambda i: (0, 0, 0)),
        pl.BlockSpec((2, 128, 128), lambda i: (0, 0, 0)),
    ]
    operands = [base, received, legendre, radial, pick, turn]
    aliases = {}
    if output is not None:
        in_specs.append(pl.BlockSpec(memory_space=pl.ANY))
        operands.append(output)
        aliases = {6: 0}

    def kernel(*refs):
        shells_kernel(first, *refs)

    return pl.pallas_call(
        kernel,
        grid=(count,),
        in_specs=in_specs,
        out_specs=pl.BlockSpec((1, rows, 128), lambda i: (first + i, 0, 0)),
        out_shape=jax.ShapeDtypeStruct((pairs_here, rows, 128), jnp.bfloat16),
        scratch_shapes=[
            pltpu.VMEM((2, 512, 512), jnp.bfloat16),
            pltpu.VMEM((TILE + 16, 256), jnp.float32),
            pltpu.VMEM((8, TILE + 16, 256), jnp.bfloat16),
            pltpu.VMEM((8 * TILE + 128, 128), jnp.float32),
            pltpu.VMEM(radial.shape, jnp.bfloat16),
            pltpu.SemaphoreType.DMA((4,)),
        ],
        input_output_aliases=aliases,
        compiler_params=pltpu.CompilerParams(vmem_limit_bytes=VMEM_LIMIT),
        cost_estimate=pl.CostEstimate(
            flops=count * 4_000_000_000, bytes_accessed=count * 5_000_000, transcendentals=0
        ),
        name="shells_piece",
    )(*operands)


def on_device(pressure, legendre, radial):
    frames, freq_dev, lat_dev, lon_count = pressure.shape
    af_count = lax.axis_size("af")
    sa_count = lax.axis_size("sa")
    pairs_here = legendre.shape[0]
    if (frames, freq_dev, lat_dev, af_count, sa_count) != (4, 8, 128, 4, 8):
        return plain_on_device(pressure, legendre, radial)
    devices = af_count * sa_count
    owner_block = lax.axis_index("af") * sa_count + lax.axis_index("sa")
    base = (owner_block * pairs_here).astype(jnp.int32).reshape(1)
    factors = radial.reshape(LDEG * 32, 128)

    lane = np.arange(256)
    freq = (lane // 32 % 4) * 8 + lane % 8
    rx = (lane // 128) * 4 + lane // 8 % 4
    same = freq[:, None] == lane[None, :] % 32
    pick = np.stack([same & (rx == k)[:, None] for k in range(8)])
    pick = jnp.asarray(pick.astype(jnp.bfloat16))
    turn = jnp.asarray(np.stack([np.eye(128), np.eye(128)[::-1]]).astype(jnp.bfloat16))

    starts = [sum(CHUNKS[:i]) for i in range(len(CHUNKS))]
    tables = [
        jnp.asarray(table_rows(lon_count, devices, pairs_here, first, count))
        for first, count in zip(starts, CHUNKS)
    ]
    spectra = [dft(table, pressure) for table in tables]
    output = None
    waiting = None
    for i, (first, count) in enumerate(zip(starts, CHUNKS)):
        if output is not None:
            spectra[i], output = lax.optimization_barrier((spectra[i], output))
        if i == len(CHUNKS) - 2:
            spectra[i:] = lax.optimization_barrier(tuple(spectra[i:]))
        spread = spectra[i].reshape(devices, 4 * count * 32, 128)
        piece = lax.all_to_all(spread, ("af", "sa"), split_axis=0, concat_axis=0, tiled=True)
        piece = piece.reshape(devices, 2, 2, count, 32, 128)
        if waiting is not None:
            output = shells_piece(base, waiting[0], legendre, factors, pick, turn, output, *waiting[1:])
        waiting = (piece, first, count)
    output = shells_piece(base, waiting[0], legendre, factors, pick, turn, output, *waiting[1:])
    return output.reshape(pairs_here, LDEG + 1, 2, frames, 128)


def solution(mesh):
    return jax.shard_map(
        on_device,
        mesh=mesh,
        in_specs=(P(None, "af", "sa", None), P(("af", "sa"), None, None), P()),
        out_specs=P(("af", "sa"), None, None, None, None),
        check_vma=False,
    )
```

```python
import math

import jax
import jax.numpy as jnp
import numpy as np
from jax import lax
from jax.experimental import pallas as pl
from jax.experimental.pallas import tpu as pltpu
from jax.sharding import PartitionSpec as P

LDEG = 1024
CHUNKS = (2, 10, 3, 1)
TILE = 1024
VMEM_LIMIT = 63 * 1024 * 1024


def order_of_column(column_count):
    column = lax.iota(jnp.int32, column_count)
    halves = column // 2
    return jnp.where(column % 2 == 0, halves, LDEG - 1 - halves)


def fourier_table(lon_count, orders):
    longitude = lax.iota(jnp.int32, lon_count)
    product = longitude[:, None] * orders[None, :] % lon_count
    phases = product.astype(jnp.float32) * (2.0 * math.pi / lon_count)
    norm_scale = 1.0 / math.sqrt(lon_count)
    return jnp.stack([jnp.cos(phases) * norm_scale, -jnp.sin(phases) * norm_scale], axis=1).astype(
        jnp.bfloat16
    )


def pair_layout(pair_index):
    column = lax.iota(jnp.int32, LDEG + 1)
    segment = (column >= LDEG - pair_index).astype(jnp.int32)
    order_here = jnp.where(segment == 1, LDEG - 1 - pair_index, pair_index)
    degree = jnp.where(segment == 1, column - 1, pair_index + column)
    parity = (degree + order_here) % 2
    return (segment, degree, parity)


def selector(segment, parity):
    branch_ids = lax.iota(jnp.int32, 2)
    seg_match = segment[..., None, None, :] == branch_ids[:, None, None]
    par_match = parity[..., None, None, :] == branch_ids[None, :, None]
    return (seg_match & par_match).astype(jnp.float32)


def harmonics(gathered, legendre, select):
    parts, per_device, frame_count, freqs, lat_count = gathered.shape
    half_count = lat_count // 2
    upper_half = gathered[..., :half_count].astype(jnp.float32)
    lower_half = jnp.flip(gathered[..., half_count:], axis=4).astype(jnp.float32)
    even_part = (upper_half + lower_half).astype(jnp.bfloat16)
    odd_part = (upper_half - lower_half).astype(jnp.bfloat16)
    folded = jnp.stack([even_part, odd_part], axis=2)
    folded = folded.reshape(parts, per_device // 2, 2, 2, frame_count, freqs, half_count)
    products = jnp.einsum(
        "rkstxfj,kqj->krstxfq", folded, legendre, preferred_element_type=jnp.float32
    )
    return jnp.sum(products * select[:, None, :, :, None, None, :], axis=(2, 3)).astype(
        jnp.bfloat16
    )


def plain_on_device(pressure, legendre, radial):
    frames, freq_dev, lat_dev, lon_count = pressure.shape
    af_count = lax.axis_size("af")
    sa_count = lax.axis_size("sa")
    per_device = LDEG // (af_count * sa_count)
    trig_table = fourier_table(lon_count, order_of_column(LDEG))
    spectra = jnp.einsum(
        "krc,xfjk->rcxfj", trig_table, pressure, preferred_element_type=jnp.float32
    ).astype(jnp.bfloat16)
    pairs_here = legendre.shape[0]
    owner_block = lax.axis_index("af") * sa_count + lax.axis_index("sa")
    pair_ids = owner_block * pairs_here + lax.iota(jnp.int32, pairs_here)
    segment, degree, parity = pair_layout(pair_ids[:, None])
    select = selector(segment, parity)
    spread = spectra.reshape(1, 2, af_count * sa_count, per_device, frames, freq_dev, lat_dev)
    piece = lax.all_to_all(spread, ("af", "sa"), split_axis=2, concat_axis=0, tiled=True)
    frame_count = piece.shape[4]
    sources = piece.reshape(af_count, sa_count, 2, per_device, frame_count, freq_dev, lat_dev)
    sources = jnp.transpose(sources, (2, 3, 4, 0, 5, 1, 6))
    gathered = sources.reshape(2, per_device, frame_count, af_count * freq_dev, sa_count * lat_dev)
    harmonic = harmonics(gathered, legendre, select)
    factors = jnp.take(radial, degree.reshape(-1), axis=0)
    factors = factors.reshape(pairs_here, LDEG + 1, radial.shape[1], radial.shape[2])
    result = jnp.einsum("krxfq,kqfs->kqrxs", harmonic, factors, preferred_element_type=jnp.float32)
    return result.astype(jnp.bfloat16)


def table_rows(lon_count, devices, pairs_here, first, count):
    pair = np.arange(devices)[:, None] * pairs_here + first + np.arange(count)[None, :]
    order = np.stack([pair, LDEG - 1 - pair], axis=1)
    product = (order[..., None].astype(np.int64) * np.arange(lon_count)) % lon_count
    phase = product.astype(np.float32) * np.float32(2.0 * math.pi / lon_count)
    scale = np.float32(1.0 / math.sqrt(lon_count))
    rows = np.stack([np.cos(phase) * scale, -np.sin(phase) * scale], axis=1)
    return rows.reshape(devices * 4 * count, lon_count).astype(jnp.bfloat16)


def dot_t(a, b):
    return lax.dot_general(a, b, (((1,), (1,)), ((), ())), preferred_element_type=jnp.float32)


def dft_kernel(table_ref, pressure_ref, out_ref, acc_ref):
    rows = table_ref.shape[0]
    frame = pl.program_id(0)
    for f in range(0, 8, 2):
        block = pressure_ref[0, f : f + 2].reshape(256, pressure_ref.shape[3])
        both = dot_t(table_ref[...], block)
        at = (frame % 2) * 8 + f
        acc_ref[pl.ds(at, rows, stride=16), :] = both[:, :128]
        acc_ref[pl.ds(at + 1, rows, stride=16), :] = both[:, 128:]

    @pl.when(frame % 2 == 1)
    def _():
        out_ref[...] = acc_ref[...].reshape(rows, 16, 128).astype(jnp.bfloat16)


def dft(table, pressure):
    rows, lon_count = table.shape
    return pl.pallas_call(
        dft_kernel,
        grid=(4,),
        in_specs=[
            pl.BlockSpec((rows, lon_count), lambda x: (0, 0), pipeline_mode=pl.Buffered(1)),
            pl.BlockSpec((1, 8, 128, lon_count), lambda x: (x, 0, 0, 0)),
        ],
        out_specs=pl.BlockSpec((rows, 16, 128), lambda x: (0, x // 2, 0)),
        out_shape=jax.ShapeDtypeStruct((rows, 32, 128), jnp.bfloat16),
        scratch_shapes=[pltpu.VMEM((rows * 16, 128), jnp.float32)],
        compiler_params=pltpu.CompilerParams(vmem_limit_bytes=VMEM_LIMIT),
        cost_estimate=pl.CostEstimate(
            flops=2 * rows * 4096 * lon_count, bytes_accessed=1 << 24, transcendentals=0
        ),
        name="dft_piece",
    )(table, pressure)


def shells_kernel(first, *refs):
    base_ref, recv_ref, leg_ref, rad_hbm_ref, pick_ref, turn_ref = refs[:6]
    out_ref, both_ref, harm_ref, copies_ref, result_ref, rad_ref, rad_sem = refs[-7:]
    pair = base_ref[0] + first + pl.program_id(0)
    bound = LDEG - pair
    quarter = rad_ref.shape[0] // 4
    radial_copies = [
        pltpu.make_async_copy(
            rad_hbm_ref.at[pl.ds(k * quarter, quarter)],
            rad_ref.at[pl.ds(k * quarter, quarter)],
            rad_sem.at[k],
        )
        for k in range(4)
    ]

    @pl.when(pl.program_id(0) == 0)
    def _():
        for copy in radial_copies:
            copy.start()

    for s in range(4):
        for seg in range(2):
            for half, sa in ((0, s), (1, 7 - s)):
                rows = [recv_ref[8 * a + sa, r, seg, 0] for r in range(2) for a in range(4)]
                turned = dot_t(turn_ref[half], jnp.concatenate(rows, axis=0))
                lanes = slice(256 * half, 256 * half + 256)
                both_ref[seg, 128 * s : 128 * s + 128, lanes] = turned.astype(jnp.bfloat16)

    own_q = (
        lax.broadcasted_iota(jnp.int32, (1, 8, 256), 2) // 32
        == lax.broadcasted_iota(jnp.int32, (1, 8, 256), 1)
    )

    def legendre_rows(rows, start, seg):
        product = jnp.dot(rows, both_ref[seg], preferred_element_type=jnp.float32)
        q = start + lax.broadcasted_iota(jnp.int32, (rows.shape[0], 256), 0)
        parity = (q + seg * pair) % 2
        north, south = product[:, :256], product[:, 256:]
        return q, north + jnp.where(parity == 0, south, -south)

    def degree(q):
        return jnp.where(q >= bound, q - 1, pair + q)

    def factors_at(degree_here):
        return rad_ref[pl.ds(pl.multiple_of(degree_here * 32, 32), 32), :]

    def fill_copies(harm):
        count = harm.shape[0]
        harm = harm.astype(jnp.bfloat16)
        for rx in range(8):
            copies = jnp.dot(harm, pick_ref[rx], preferred_element_type=jnp.float32)
            own = jnp.where(own_q, copies.reshape(count // 8, 8, 256), 0.0)
            copies_ref[rx, 0:count] = own.reshape(count, 256).astype(jnp.bfloat16)

    def radial_block(block, slab):
        rows = [copies_ref[rx, 16 * block : 16 * block + 16] for rx in range(8)]
        rows = jnp.concatenate(rows, axis=0)
        result = jnp.dot(rows, slab, preferred_element_type=jnp.float32)
        for rx in range(8):
            for half in range(2):
                at = 128 * block + 64 * half + rx
                part = result[16 * rx + 8 * half :, 128 * half : 128 * half + 128]
                result_ref[pl.ds(at, 8, stride=8), :] = part[:8]

    def columns(start, rows, slabs, first_tile):
        count = rows.shape[0]

        half = LDEG // 2
        _, near = legendre_rows(rows, start, 0)
        q, far = legendre_rows(rows[half:], start + half, 1)
        harm_ref[0:half] = near[:half]
        harm_ref[half:count] = jnp.where(q >= bound, far, near[half:])

        fill_copies(harm_ref[0:count])
        if first_tile:

            @pl.when(pl.program_id(0) == 0)
            def _():
                for copy in radial_copies:
                    copy.wait()

        for block, slab in enumerate(slabs):
            radial_block(block, slab())
        out_rows = min(8 * count, 8 * (LDEG + 1) - 8 * (LDEG - TILE))
        out_ref[0, 8 * start : 8 * start + out_rows, :] = result_ref[0:out_rows].astype(jnp.bfloat16)

    def slab_of(start, block):
        def slab():
            q = start + 16 * block
            halves = [[factors_at(degree(q + 8 * half + k)) for k in range(8)] for half in range(2)]
            return jnp.concatenate([jnp.concatenate(h, axis=0) for h in halves], axis=1)

        return slab

    for start in range(0, LDEG - TILE, TILE):
        rows = leg_ref[0, start : start + TILE, :]
        columns(start, rows, [slab_of(start, block) for block in range(TILE // 16)], start == 0)

    start = LDEG - TILE
    last = leg_ref[0, LDEG : LDEG + 1, :].astype(jnp.float32)
    last = jnp.broadcast_to(last, (16, 512)).astype(jnp.bfloat16)
    rows = jnp.concatenate([leg_ref[0, start:LDEG, :], last], axis=0)
    slabs = [slab_of(start, block) for block in range(TILE // 16)]
    slabs.append(lambda: jnp.tile(factors_at(LDEG - 1), (8, 2)))
    columns(start, rows, slabs, start == 0)


def shells_piece(base, received, legendre, radial, pick, turn, output, first, count):
    pairs_here = legendre.shape[0]
    rows = 8 * (LDEG + 1)
    in_specs = [
        pl.BlockSpec(memory_space=pltpu.SMEM),
        pl.BlockSpec((32, 2, 2, 1, 32, 128), lambda i: (0, 0, 0, i, 0, 0)),
        pl.BlockSpec((1, LDEG + 1, 512), lambda i: (first + i, 0, 0)),
        pl.BlockSpec(memory_space=pl.ANY),
        pl.BlockSpec((8, 256, 256), lambda i: (0, 0, 0)),
        pl.BlockSpec((2, 128, 128), lambda i: (0, 0, 0)),
    ]
    operands = [base, received, legendre, radial, pick, turn]
    aliases = {}
    if output is not None:
        in_specs.append(pl.BlockSpec(memory_space=pl.ANY))
        operands.append(output)
        aliases = {6: 0}

    def kernel(*refs):
        shells_kernel(first, *refs)

    return pl.pallas_call(
        kernel,
        grid=(count,),
        in_specs=in_specs,
        out_specs=pl.BlockSpec((1, rows, 128), lambda i: (first + i, 0, 0)),
        out_shape=jax.ShapeDtypeStruct((pairs_here, rows, 128), jnp.bfloat16),
        scratch_shapes=[
            pltpu.VMEM((2, 512, 512), jnp.bfloat16),
            pltpu.VMEM((TILE + 16, 256), jnp.float32),
            pltpu.VMEM((8, TILE + 16, 256), jnp.bfloat16),
            pltpu.VMEM((8 * TILE + 128, 128), jnp.float32),
            pltpu.VMEM(radial.shape, jnp.bfloat16),
            pltpu.SemaphoreType.DMA((4,)),
        ],
        input_output_aliases=aliases,
        compiler_params=pltpu.CompilerParams(vmem_limit_bytes=VMEM_LIMIT),
        cost_estimate=pl.CostEstimate(
            flops=count * 4_000_000_000, bytes_accessed=count * 5_000_000, transcendentals=0
        ),
        name="shells_piece",
    )(*operands)


def on_device(pressure, legendre, radial):
    frames, freq_dev, lat_dev, lon_count = pressure.shape
    af_count = lax.axis_size("af")
    sa_count = lax.axis_size("sa")
    pairs_here = legendre.shape[0]
    if (frames, freq_dev, lat_dev, af_count, sa_count) != (4, 8, 128, 4, 8):
        return plain_on_device(pressure, legendre, radial)
    devices = af_count * sa_count
    owner_block = lax.axis_index("af") * sa_count + lax.axis_index("sa")
    base = (owner_block * pairs_here).astype(jnp.int32).reshape(1)
    factors = radial.reshape(LDEG * 32, 128)

    lane = np.arange(256)
    freq = (lane // 32 % 4) * 8 + lane % 8
    rx = (lane // 128) * 4 + lane // 8 % 4
    same = freq[:, None] == lane[None, :] % 32
    pick = np.stack([same & (rx == k)[:, None] for k in range(8)])
    pick = jnp.asarray(pick.astype(jnp.bfloat16))
    turn = jnp.asarray(np.stack([np.eye(128), np.eye(128)[::-1]]).astype(jnp.bfloat16))

    starts = [sum(CHUNKS[:i]) for i in range(len(CHUNKS))]
    tables = [
        jnp.asarray(table_rows(lon_count, devices, pairs_here, first, count))
        for first, count in zip(starts, CHUNKS)
    ]
    spectra = [dft(table, pressure) for table in tables]
    output = None
    waiting = None
    for i, (first, count) in enumerate(zip(starts, CHUNKS)):
        if output is not None:
            spectra[i], output = lax.optimization_barrier((spectra[i], output))
        if i == len(CHUNKS) - 2:
            spectra[i:] = lax.optimization_barrier(tuple(spectra[i:]))
        spread = spectra[i].reshape(devices, 4 * count * 32, 128)
        piece = lax.all_to_all(spread, ("af", "sa"), split_axis=0, concat_axis=0, tiled=True)
        piece = piece.reshape(devices, 2, 2, count, 32, 128)
        if waiting is not None:
            output = shells_piece(base, waiting[0], legendre, factors, pick, turn, output, *waiting[1:])
        waiting = (piece, first, count)
    output = shells_piece(base, waiting[0], legendre, factors, pick, turn, output, *waiting[1:])
    return output.reshape(pairs_here, LDEG + 1, 2, frames, 128)


def solution(mesh):
    return jax.shard_map(
        on_device,
        mesh=mesh,
        in_specs=(P(None, "af", "sa", None), P(("af", "sa"), None, None), P()),
        out_specs=P(("af", "sa"), None, None, None, None),
        check_vma=False,
    )
```
